128 devices in a mesh: dp: 32 (over x, y_lo, z), tensor: 4 (over y_hi, core).
Axes of the slice: x: 4, y: 4 (y_hi: 2, y_lo: 2; y = y_hi * 2 + y_lo), z: 4, core: 2. Of those that a mesh axis runs over, the one named last changes fastest.
Arguments:
- tokens_in: bfloat16 [16384, 1152], P(('dp', 'tensor')), may hold values from -24 to 24
- lengths: int32 [32, 8], P('dp'), may hold values from 1 to 505, as said below
- att_in_gain: bfloat16 [1152], P('dp'), may hold values from -0.5 to 0.5
- query_weight: bfloat16 [1152, 1024], P('dp', 'tensor'), may hold values from -0.1875 to 0.1875
- key_weight: bfloat16 [1152, 256], P('dp'), may hold values from -0.1875 to 0.1875
- value_weight: bfloat16 [1152, 256], P('dp'), may hold values from -0.1875 to 0.1875
- query_gain: bfloat16 [256], P('dp'), may hold values from -0.5 to 0.5
- key_gain: bfloat16 [256], P('dp'), may hold values from -0.5 to 0.5
- out_weight: bfloat16 [1024, 1152], P('tensor', 'dp'), may hold values from -0.1875 to 0.1875
- att_out_gain: bfloat16 [1152], P('dp'), may hold values from -0.5 to 0.5
- ffw_in_gain: bfloat16 [1152], P('dp'), may hold values from -0.5 to 0.5
- gate_weight: bfloat16 [1152, 6912], P('dp', 'tensor'), may hold values from -0.1875 to 0.1875
- up_weight: bfloat16 [1152, 6912], P('dp', 'tensor'), may hold values from -0.1875 to 0.1875
- down_weight: bfloat16 [6912, 1152], P('tensor', 'dp'), may hold values from -0.078125 to 0.078125
- ffw_out_gain: bfloat16 [1152], P('dp'), may hold values from -0.5 to 0.5
- cotangent: bfloat16 [16384, 1152], P(('dp', 'tensor')), may hold values from -24 to 24
Outputs:
- mixed_out: bfloat16 [16384, 1152], P(('dp', 'tensor'))
- tokens_grad: float32 [16384, 1152], P(('dp', 'tensor'))
- att_in_gain_grad: float32 [1152], P('dp')
- query_weight_grad: float32 [1152, 1024], P('dp', 'tensor')
- key_weight_grad: float32 [1152, 256], P('dp')
- value_weight_grad: float32 [1152, 256], P('dp')
- query_gain_grad: float32 [256], P('dp')
- key_gain_grad: float32 [256], P('dp')
- out_weight_grad: float32 [1024, 1152], P('tensor', 'dp')
- att_out_gain_grad: float32 [1152], P('dp')
- ffw_in_gain_grad: float32 [1152], P('dp')
- gate_weight_grad: float32 [1152, 6912], P('dp', 'tensor')
- up_weight_grad: float32 [1152, 6912], P('dp', 'tensor')
- down_weight_grad: float32 [6912, 1152], P('tensor', 'dp')
- ffw_out_gain_grad: float32 [1152], P('dp')
The draws below stay inside these ranges and needn't reach their ends.
Inputs may be any that keep to these rules, and one draw needn't show every extreme that they name: Row g gives, in order, the lengths of the 8 documents packed into data group g's 512 tokens: each row sums to 512, and its longest document has 386 tokens or more.
All inputs are finite; a program needn't handle non-finite values.
Results may differ from the reference program's by a relative error of at most 0.04.
Values may be sent and summed in bfloat16 or wider, within the bound.
A program may use at most 128 MiB of HBM per device.

```python
import math
import jax
import jax.numpy as jnp
from jax import lax

D = 1152
HEADS = 4
HD = 256
FF = 6912
TOK_DEV = 128
DOCS = 8
TOK_GRP = 512
TOKENS = 16384
N_DP = 32


def draw_lengths(key, part):
    key = jax.random.fold_in(key, 7)
    key_short, key_row, key_shift = jax.random.split(key, 3)
    groups = TOKENS // TOK_GRP
    short_most = (TOK_DEV - 2) // (DOCS - 1)
    shorter = jax.random.randint(key_short, (groups, DOCS - 1), 1, short_most + 1)
    chosen = jax.random.randint(key_row, (), 0, groups)
    row_ids = jnp.arange(groups)[:, None]
    shorter = jnp.where(row_ids == chosen, 1, shorter)
    longest = TOK_GRP - jnp.sum(shorter, axis=1, keepdims=True)
    table = jnp.concatenate([longest, shorter], axis=1)
    shift = jax.random.randint(key_shift, (groups, 1), 0, DOCS)
    order = (jnp.arange(DOCS)[None, :] - shift) % DOCS
    return jnp.take_along_axis(table, order, axis=1).astype(jnp.int32)


def spiked(drawn, key, source, target, blocks, factor):
    owner, partner = [(jnp.arange(drawn.shape[dim]) // (drawn.shape[dim] // blocks)).reshape([-1 if axis == dim else 1 for axis in range(drawn.ndim)]) for dim in (source, target)]
    chosen = jax.random.permutation(key, blocks)[partner]
    strong = (owner == chosen) | (owner == (partner + blocks // 2) % blocks)
    return jnp.where(strong, factor * drawn, drawn)


def block_levels(key, extent, pieces, low, largest):
    def one(axis_at, shards_of):
        steps = jax.random.uniform(jax.random.fold_in(jax.random.fold_in(key, 6), axis_at), (shards_of,), jnp.float32, low / len(pieces), largest / len(pieces))
        return jnp.repeat(jnp.exp(steps), extent[axis_at] // shards_of).reshape((-1,) + (1,) * (len(extent) - axis_at - 1))

    factor_of = one(*pieces[0])
    for cut in pieces[1:]:
        factor_of = factor_of * one(*cut)
    return factor_of


def bell_draw(stream_key, dims, deviation, most, shards=(), kind=jnp.bfloat16):
    loudness = block_levels(stream_key, dims, shards, -0.22, 0.18) if shards else 1.0
    entries = jax.random.normal(stream_key, dims, jnp.float32) * deviation * loudness
    return jnp.minimum(jnp.maximum(entries, -most), most).astype(kind)


def bell_draw_with(own_key, shape, deviation, limit, pieces, heavy, kind=jnp.bfloat16):
    entries = deviation * jax.random.normal(own_key, shape, jnp.float32)
    if pieces:
        entries = entries * block_levels(own_key, shape, pieces, -0.22, 0.18)
    return jnp.clip(spiked(entries, jax.random.fold_in(own_key, 3), *heavy), -limit, limit).astype(kind)


def setup_inputs(seed: int = 0) -> dict:
    arg_keys = jax.random.split(jax.random.key(seed), 17)
    tokens_in = bell_draw_with(arg_keys[0], (TOKENS, D), 1.0, 24.0, ((0, 128),), (0, 1, 128, 5.5))
    lengths = draw_lengths(jax.random.fold_in(arg_keys[16], 71), 0)
    att_in_gain = jnp.clip(jax.random.uniform(arg_keys[2], (D,), jnp.float32, -0.5, 0.5) * block_levels(arg_keys[2], (D,), ((0, 32),), -0.4, 0.0), -0.5, 0.5).astype(jnp.bfloat16)
    query_weight = bell_draw(arg_keys[3], (D, HEADS * HD), D ** -0.5, 0.1875, ((0, 32), (1, 4)))
    key_weight = bell_draw(arg_keys[4], (D, HD), D ** -0.5, 0.1875, ((0, 32),))
    value_weight = bell_draw(arg_keys[5], (D, HD), D ** -0.5, 0.1875, ((0, 32),))
    query_gain = jnp.clip(jax.random.uniform(arg_keys[6], (HD,), jnp.float32, -0.5, 0.5) * block_levels(arg_keys[6], (HD,), ((0, 32),), -0.4, 0.0), -0.5, 0.5).astype(jnp.bfloat16)
    key_gain = jnp.clip(jax.random.uniform(arg_keys[7], (HD,), jnp.float32, -0.5, 0.5) * block_levels(arg_keys[7], (HD,), ((0, 32),), -0.4, 0.0), -0.5, 0.5).astype(jnp.bfloat16)
    out_weight = bell_draw(arg_keys[8], (HEADS * HD, D), (HEADS * HD) ** -0.5, 0.1875, ((0, 4), (1, 32)))
    att_out_gain = jnp.clip(jax.random.uniform(arg_keys[9], (D,), jnp.float32, -0.5, 0.5) * block_levels(arg_keys[9], (D,), ((0, 32),), -0.4, 0.0), -0.5, 0.5).astype(jnp.bfloat16)
    ffw_in_gain = jnp.clip(jax.random.uniform(arg_keys[10], (D,), jnp.float32, -0.5, 0.5) * block_levels(arg_keys[10], (D,), ((0, 32),), -0.4, 0.0), -0.5, 0.5).astype(jnp.bfloat16)
    gate_weight = bell_draw(arg_keys[11], (D, FF), D ** -0.5, 0.1875, ((0, 32), (1, 4)))
    up_weight = bell_draw(arg_keys[12], (D, FF), D ** -0.5, 0.1875, ((0, 32), (1, 4)))
    down_weight = bell_draw(arg_keys[13], (FF, D), FF ** -0.5, 0.078125, ((0, 4), (1, 32)))
    ffw_out_gain = jnp.clip(jax.random.uniform(arg_keys[14], (D,), jnp.float32, -0.5, 0.5) * block_levels(arg_keys[14], (D,), ((0, 32),), -0.4, 0.0), -0.5, 0.5).astype(jnp.bfloat16)
    cotangent = bell_draw_with(arg_keys[15], (TOKENS, D), 1.0, 24.0, ((0, 128),), (0, 1, 128, 5.5))
    return dict(tokens_in=tokens_in, lengths=lengths, att_in_gain=att_in_gain, query_weight=query_weight, key_weight=key_weight, value_weight=value_weight, query_gain=query_gain, key_gain=key_gain, out_weight=out_weight, att_out_gain=att_out_gain, ffw_in_gain=ffw_in_gain, gate_weight=gate_weight, up_weight=up_weight, down_weight=down_weight, ffw_out_gain=ffw_out_gain, cotangent=cotangent)


EPS = 1e-06
THETA = 1000000.0
NEGATIVE = -1e+30
HIGHEST = lax.Precision.HIGHEST

@jax.custom_vjp
def low(v):
    return lax.optimization_barrier(v.astype(jnp.bfloat16)).astype(jnp.float32)

@jax.custom_vjp
def low_back(v):
    return v

def low_keep(v):
    return (low(v), None)

def low_pass(kept, grad):
    return (grad,)

def back_keep(v):
    return (v, None)

def back_low(kept, grad):
    return (low(grad),)
low.defvjp(low_keep, low_pass)
low_back.defvjp(back_keep, back_low)

def matmul(former, latter):
    return jnp.dot(former, latter, precision=HIGHEST, preferred_element_type=jnp.float32)

def normed(vector, factor):
    return vector * lax.rsqrt(lax.optimization_barrier(jnp.mean(vector * vector, axis=-1, keepdims=True)) + EPS) * (1.0 + factor)

def layout(lengths_row, row_count):
    doc_ends = jnp.cumsum(lengths_row).astype(jnp.int32)
    doc_starts = doc_ends - lengths_row
    token_index = jnp.arange(row_count, dtype=jnp.int32)
    segment = lax.optimization_barrier(jnp.sum((token_index[:, None] >= doc_ends[None, :]).astype(jnp.int32), axis=1))
    doc_ids = jnp.arange(lengths_row.shape[0], dtype=jnp.int32)
    doc_begin = lax.optimization_barrier(jnp.sum(jnp.where(segment[:, None] == doc_ids[None, :], doc_starts[None, :], 0), axis=1))
    return (segment, (token_index - doc_begin).astype(jnp.int32))

def rope_tables(position, head_size):
    half_size = head_size // 2
    frequency = jnp.exp(jnp.arange(half_size, dtype=jnp.float32) * (-2.0 * math.log(THETA) / head_size))
    angles = position.astype(jnp.float32)[:, None] * frequency[None, :]
    return (jnp.cos(angles), jnp.sin(angles))

def rotate(vector, cosine, sine_part):
    half_size = vector.shape[-1] // 2
    leading = vector[..., :half_size]
    trailing = vector[..., half_size:]
    return jnp.concatenate([leading * cosine - trailing * sine_part, trailing * cosine + leading * sine_part], axis=-1)

def activate(gate_proj, up_proj):
    return jax.nn.gelu(gate_proj, approximate=True) * up_proj

def group_fn(weights, group_x, segment, position):
    att_in_gain, query_weight, key_weight, value_weight, query_gain, key_gain, out_weight, att_out_gain, ffw_in_gain, gate_weight, up_weight, down_weight, ffw_out_gain = weights
    row_count = group_x.shape[0]
    first_normed = low(normed(group_x, att_in_gain))
    query_raw = low_back(matmul(first_normed, query_weight)).reshape(row_count, HEADS, HD)
    key_raw = low_back(matmul(first_normed, key_weight))
    value_b = low(low_back(matmul(first_normed, value_weight)))
    cosine, sine_part = rope_tables(position, HD)
    query_b = low(rotate(normed(query_raw, query_gain), cosine[:, None, :], sine_part[:, None, :]) * HD ** (-0.5))
    key_b = low(rotate(normed(key_raw, key_gain), cosine, sine_part))
    scores = low_back(jnp.einsum('qhd,kd->hqk', query_b, key_b, precision=HIGHEST))
    token_index = jnp.arange(row_count)
    allowed = (segment[:, None] == segment[None, :]) & (token_index[None, :] <= token_index[:, None])
    shares_b = low(jax.nn.softmax(jnp.where(allowed[None], scores, NEGATIVE), axis=-1))
    attended = low(low_back(jnp.einsum('hqk,kd->qhd', shares_b, value_b, precision=HIGHEST)))
    att_raw = low_back(matmul(attended.reshape(row_count, HEADS * HD), out_weight))
    middle = group_x + normed(att_raw, att_out_gain)
    second_normed = low(normed(middle, ffw_in_gain))
    gate_proj = low_back(matmul(second_normed, gate_weight))
    up_proj = low_back(matmul(second_normed, up_weight))
    hidden = low(activate(gate_proj, up_proj))
    ffn_raw = low_back(matmul(hidden, down_weight))
    return middle + normed(ffn_raw, ffw_out_gain)

def reference(tokens_in, lengths, att_in_gain, query_weight, key_weight, value_weight, query_gain, key_gain, out_weight, att_out_gain, ffw_in_gain, gate_weight, up_weight, down_weight, ffw_out_gain, cotangent):
    weights = tuple((member.astype(jnp.float32) for member in (att_in_gain, query_weight, key_weight, value_weight, query_gain, key_gain, out_weight, att_out_gain, ffw_in_gain, gate_weight, up_weight, down_weight, ffw_out_gain)))
    inputs = tokens_in.astype(jnp.float32).reshape(N_DP, TOK_GRP, D)
    segment, position = jax.vmap(lambda lengths_row: layout(lengths_row, TOK_GRP))(lengths)
    block_fn = jax.checkpoint(group_fn)

    def forward(group_inputs, weight_set):
        return lax.map(lambda packed: block_fn(weight_set, packed[0], packed[1], packed[2]), (group_inputs, segment, position))
    outputs, pullback = jax.vjp(forward, inputs, weights)
    inputs_grad, weight_grads = pullback(cotangent.astype(jnp.float32).reshape(N_DP, TOK_GRP, D))
    att_in_gain_grad, query_weight_grad, key_weight_grad, value_weight_grad, query_gain_grad, key_gain_grad, out_weight_grad, att_out_gain_grad, ffw_in_gain_grad, gate_weight_grad, up_weight_grad, down_weight_grad, ffw_out_gain_grad = weight_grads
    return (outputs.reshape(TOKENS, D).astype(jnp.bfloat16), inputs_grad.reshape(TOKENS, D), att_in_gain_grad, query_weight_grad, key_weight_grad, value_weight_grad, query_gain_grad, key_gain_grad, out_weight_grad, att_out_gain_grad, ffw_in_gain_grad, gate_weight_grad, up_weight_grad, down_weight_grad, ffw_out_gain_grad)
```

```python
import math
from types import SimpleNamespace

import jax
import jax.numpy as jnp
from jax import lax
from jax.experimental import pallas as pl
from jax.experimental.pallas import tpu as pltpu
from jax.sharding import PartitionSpec as P

EPS = 1e-06
THETA = 1000000.0
NEGATIVE = -1e30
MESH = pl.DeviceIdType.MESH
BF = jnp.bfloat16
F32 = jnp.float32
D = 1152
MAIN = 32
TAIL = 16
HALF = 864
HPAD = 896
CF = 3 * HPAD
CA = 1024
TA = 384
LIMIT = 58 * 1024 * 1024
CU = 2 * HPAD
WIDE = D + 256
GELU = math.sqrt(2.0 / math.pi)


def matmul(former, latter):
    return jnp.dot(former, latter, preferred_element_type=jnp.float32)


def left_inner(former, latter):
    return lax.dot_general(
        former, latter, (((0,), (0,)), ((), ())), preferred_element_type=jnp.float32
    )


def right_inner(former, latter):
    return lax.dot_general(
        former, latter, (((1,), (1,)), ((), ())), preferred_element_type=jnp.float32
    )


def place():
    d = lax.axis_index("dp")
    t = lax.axis_index("tensor")
    return d // 8, (d // 4) % 2, d % 4, t // 2, t % 2


def device(x, yl, z, yh, core):
    return {"dp": (x * 2 + yl) * 4 + z, "tensor": yh * 2 + core}


def neighbours():
    x, yl, z, yh, c = place()
    y = yh * 2 + yl

    def along_a(step):
        return device((x + yl * step) % 4, yl, (z + (1 - yl) * step) % 4, yh, c)

    def along_b(step):
        return device((x + (1 - yl) * step) % 4, yl, (z + yl * step) % 4, yh, c)

    up, down = (y + 1) % 4, (y + 3) % 4
    return dict(
        ap=along_a(1),
        am=along_a(3),
        ao=along_a(2),
        bp=along_b(1),
        bm=along_b(3),
        bo=along_b(2),
        pair=device(x, 1 - yl, z, yh, c),
        twin=device(x, yl, z, yh, 1 - c),
        far=device(x, yl, z, 1 - yh, c),
        fartwin=device(x, yl, z, 1 - yh, 1 - c),
        pairtwin=device(x, 1 - yl, z, yh, 1 - c),
        pairfar=device(x, 1 - yl, z, 1 - yh, c),
        opposite=device(x, 1 - yl, z, 1 - yh, 1 - c),
        yp=device(x, up % 2, z, up // 2, c),
        ym=device(x, down % 2, z, down // 2, c),
    )


GROUP = ("twin", "far", "fartwin", "pairtwin", "pairfar", "opposite")


def greet(names):
    near = neighbours()
    barrier = pltpu.get_barrier_semaphore()
    for name in names:
        pl.semaphore_signal(barrier, inc=1, device_id=near[name], device_id_type=MESH)
    return lambda: pl.semaphore_wait(barrier, len(names))


class Links:
    def __init__(self, send, recv):
        self.send, self.recv, self.near, self.sent = send, recv, neighbours(), []
        self.count = 0

    def copy(self, source, target, name):
        at = self.count
        self.count += 1
        made = pltpu.make_async_remote_copy(
            src_ref=source,
            dst_ref=target,
            send_sem=self.send.at[at],
            recv_sem=self.recv.at[at],
            device_id=self.near[name],
            device_id_type=MESH,
        )
        made.start()
        self.sent.append(made)
        return made

    def settle(self, *copies):
        for made in copies:
            made.wait_send()
            self.sent = [other for other in self.sent if other is not made]

    def drain(self):
        for made in self.sent:
            made.wait_send()
        self.sent = []


def rows(ref, start, count, unit=16):
    return ref.at[pl.ds(pl.multiple_of(start, unit), count), :]


def keep(local, source, target, at):
    made = pltpu.make_async_copy(source, target, local.at[at])
    made.start()
    return made


def add_rows(target, target_at, sources, count):
    step = 64 if count % 64 == 0 else min(count, 32)

    @pl.loop(0, count, step=step)
    def _(at):
        total = None
        for ref, first in sources:
            term = ref[pl.ds(pl.multiple_of(first + at, 16), step), :].astype(F32)
            total = term if total is None else total + term
        target[pl.ds(pl.multiple_of(target_at + at, 16), step), :] = total.astype(target.dtype)


class Spread:
    def __init__(self, links, ref, first, me, size, half, plus, minus, _):
        self.links, self.ref, self.first, self.me = links, ref, first, me
        self.size, self.half, self.plus, self.minus = size, half, plus, minus
        mine = rows(ref, first(me), size)
        self.a = links.copy(mine, mine, plus)
        self.b = links.copy(mine, mine, minus)

    def forward(self):
        self.a.wait_recv()
        at = self.first((self.me + 3) % 4)
        part = rows(self.ref, at, self.half)
        self.c = self.links.copy(part, part, self.plus)
        self.b.wait_recv()
        self.d = None
        if self.half < self.size:
            at = self.first((self.me + 1) % 4)
            part = rows(self.ref, at + self.half, self.size - self.half)
            self.d = self.links.copy(part, part, self.minus)

    def finish(self):
        self.c.wait_recv()
        if self.d is not None:
            self.d.wait_recv()


class SpreadAtOnce:
    def __init__(self, links, ref, first, me, size, _, *sides):
        mine = rows(ref, first(me), size)
        self.copies = [links.copy(mine, mine, side) for side in sides]

    def forward(self):
        pass

    def finish(self):
        for made in self.copies:
            made.wait_recv()


SIDES = (("ap", "am", "ao"), ("bp", "bm", "bo"))


def roles():
    x, yl, z, _, _ = place()
    a, b = z + yl * (x - z), x + yl * (z - x)
    return (
        (yl * 16, b, a, SIDES[1], SIDES[0]),
        ((1 - yl) * 16, a, b, SIDES[0], SIDES[1]),
    )


def tail_picks(at):
    row = lax.broadcasted_iota(jnp.int32, (128, 512), 0)
    column = lax.broadcasted_iota(jnp.int32, (128, 512), 1)
    return (column == (row >> 2) * 16 + at * 4 + (row & 3)).astype(F32).astype(BF)


class Collect:
    def __init__(self, links, ref, first, me, size, half, plus, minus, _, room):
        self.links, self.ref, self.first, self.me = links, ref, first, me
        self.size, self.half, self.plus, self.minus = size, half, plus, minus
        self.one, self.other, self.low, self.high = room
        rest = size - half
        far, after, before = first((me + 2) % 4), first((me + 1) % 4), first((me + 3) % 4)
        self.a = links.copy(rows(ref, far, half), self.one, plus)
        if rest:
            self.b = links.copy(rows(ref, far + half, rest), self.other, minus)
            self.c = links.copy(rows(ref, after + half, rest), rows(self.low, half, rest), plus)
        self.d = links.copy(rows(ref, before, half), rows(self.high, 0, half), minus)

    def forward(self):
        rest = self.size - self.half
        self.a.wait_recv()
        after = self.first((self.me + 1) % 4)
        add_rows(self.one, 0, [(self.one, 0), (self.ref, after)], self.half)
        self.e = self.links.copy(self.one, rows(self.low, 0, self.half), self.plus)
        if rest:
            self.b.wait_recv()
            before = self.first((self.me + 3) % 4) + self.half
            add_rows(self.other, 0, [(self.other, 0), (self.ref, before)], rest)
            self.f = self.links.copy(self.other, rows(self.high, self.half, rest), self.minus)

    def finish(self, target, target_at):
        self.d.wait_recv()
        self.e.wait_recv()
        if self.size > self.half:
            self.c.wait_recv()
            self.f.wait_recv()
        add_rows(
            target,
            target_at,
            [(self.ref, self.first(self.me)), (self.low, 0), (self.high, 0)],
            self.size,
        )


class CollectAtOnce:
    def __init__(self, links, ref, first, me, size, _, plus, minus, opposite, room):
        self.ref, self.first, self.me, self.size, self.room = ref, first, me, size, room
        self.copies = [
            links.copy(rows(ref, first((me + step) % 4), size), target, side)
            for step, target, side in ((1, room[2], plus), (3, room[3], minus), (2, room[0], opposite))
        ]

    def forward(self):
        pass

    def finish(self, target, target_at):
        for made in self.copies:
            made.wait_recv()
        terms = [(self.ref, self.first(self.me))] + [(self.room[at], 0) for at in (2, 3, 0)]
        add_rows(target, target_at, terms, self.size)


def room_shapes(size, half, columns):
    return [
        pltpu.VMEM((half, columns), BF),
        pltpu.VMEM((max(size - half, 16), columns), BF),
        pltpu.VMEM((size, columns), BF),
        pltpu.VMEM((size, columns), BF),
    ]


KINDS = ((MAIN, CA), (TAIL, TA), (MAIN, CU), (MAIN, HPAD), (TAIL, HPAD))
SHAPES = dict(
    watt=((D, CA), BF),
    wffn=((D, CF), BF),
    tatt=((512, TA), BF),
    tffn=((512, HPAD), BF),
    raw=((512, D), BF),
    rows1=((512, D), BF),
    gains=((16, WIDE), F32),
    ggains=((16, WIDE), F32),
    qkraw=((512, 512), F32),
    vb=((512, 256), BF),
    qb=((512, 256), BF),
    kb=((512, 256), BF),
    prob=((512, 512), F32),
    attd=((512, 256), BF),
    other=((128, D), BF),
    near=((128, D), BF),
    over=((128, D), BF),
    attraw=((128, D), F32),
    middle=((128, D), F32),
    summed=((128, D), F32),
    midgrad=((128, D), F32),
    block=((128, D), BF),
    rows2=((1024, D), BF),
    back=((1024, D), BF),
    ab=((1024, CU), BF),
    hid=((1024, HPAD), BF),
    terms=((1024, D), BF),
    near8=((512, D), BF),
    one8=((64, D), BF),
    other8=((64, D), BF),
    low8=((128, D), BF),
    high8=((128, D), BF),
    gatt=((D, CA), BF),
    shuffle=((D, D), BF),
    tokens=((128, D), BF),
    cotangent=((128, D), BF),
    cosine=((512, 128), F32),
    sine=((512, 128), F32),
    begins=((512, 128), jnp.int32),
    att_main=((MAIN, CA), BF),
    att_tail=((TAIL, TA), BF),
    att_tail32=((TAIL, TA), F32),
    ffn_main=((2, MAIN, CF), BF),
    ffn_tail=((2, TAIL, HPAD), BF),
    ffn_tail32=((2 * TAIL, HPAD), F32),
    fold=((WIDE, 128), BF),
    masks=((512, WIDE), BF),
    gdown=((D, HPAD), BF),
    shared=((6 * MAIN, 512), BF),
    shared_tail=((6 * TAIL, TA), BF),
)
for at, (unit, columns) in enumerate(KINDS):
    SHAPES["sum%d" % at] = ((2 * unit, columns), BF)
    SHAPES["swap%d" % at] = ((unit, columns), BF)
    for level, (size, half) in enumerate(((4 * unit, 2 * unit), (unit, 16)) * 2):
        for side, count in enumerate(
            (size if unit == TAIL else half, max(size - half, 16), size, size)
        ):
            SHAPES["room%d%d%d" % (at, level, side)] = ((count, columns), BF)
NAMES = tuple(SHAPES)


def make_gain_maps(v):
    column = lax.broadcasted_iota(jnp.int32, (WIDE, 128), 0)
    lane = lax.broadcasted_iota(jnp.int32, (WIDE, 128), 1)
    inside = jnp.where(
        column < 1024, column & 31, jnp.where(column < D, 32 + (column & 3), column & 7)
    )
    v.fold[...] = (lane == inside).astype(F32).astype(BF)
    wide = lax.broadcasted_iota(jnp.int32, (1, WIDE), 1)
    held = jnp.where(
        wide < 1024, wide >> 5, jnp.where(wide < D, (wide - 1024) >> 2, ((wide - D) >> 3) + 32)
    )

    @pl.loop(0, 512, step=64)
    def _(at):
        slot = (lax.broadcasted_iota(jnp.int32, (64, 1), 0) + at) >> 4
        part, outer, inner = slot >> 4, (slot >> 2) & 3, slot & 3
        owner = jnp.where(part == 0, outer * 8 + inner, inner * 8 + 4 + outer)
        mask = (held == slot) | (held == owner + 32)
        v.masks[chunk_rows(at, 64), :] = mask.astype(F32).astype(BF)


def row_picks():
    row = lax.broadcasted_iota(jnp.int32, (16, 128), 0)
    column = lax.broadcasted_iota(jnp.int32, (16, 128), 1)
    return ((column & 15) == row).astype(F32).astype(BF)


def root(vector):
    return lax.rsqrt(jnp.mean(vector * vector, axis=-1, keepdims=True) + EPS)


def norm_back(vector, scale, grad):
    r = root(vector)
    weighted = grad * scale
    inner = jnp.mean(vector * weighted, axis=-1, keepdims=True)
    return r * weighted - vector * (r * r * r * inner), jnp.sum(
        grad * vector * r, axis=0, keepdims=True
    )


def turn(vector, cosine, sine_part):
    leading, trailing = vector[:, :128], vector[:, 128:]
    return jnp.concatenate(
        [leading * cosine - trailing * sine_part, trailing * cosine + leading * sine_part], axis=1
    )


def chunk_rows(start, count):
    return pl.ds(pl.multiple_of(start, 16), count)


class FourGather:
    def __init__(self, links, block, out, local, at):
        _, _, _, yh, core = place()
        self.links, self.out = links, out
        self.theirs = (1 - yh) * 2 + core
        mine = rows(out, (yh * 2 + core) * 128, 128)
        self.kept = keep(local, block, mine, at)
        self.a = links.copy(block, mine, "far")
        self.b = links.copy(block, mine, "twin")

    def forward(self):
        self.a.wait_recv()
        theirs = rows(self.out, self.theirs * 128, 128)
        self.c = self.links.copy(theirs, theirs, "twin")

    def finish(self):
        self.kept.wait()
        self.b.wait_recv()
        self.c.wait_recv()


class FourReduce:
    def __init__(self, links, term, v):
        _, _, _, yh, core = place()
        self.links, self.term, self.v = links, term, v
        self.mine, self.across = yh * 2 + core, (1 - yh) * 2 + core
        part = v.terms
        part[0:128, :] = term((1 - yh) * 2 + 1 - core).astype(BF)
        self.a = links.copy(rows(part, 0, 128), v.other, "twin")
        part[128:256, :] = term(yh * 2 + 1 - core).astype(BF)
        self.b = links.copy(rows(part, 128, 128), v.near, "twin")

    def middle(self):
        part, v = self.v.terms, self.v
        part[256:384, :] = self.term(self.across).astype(BF)
        self.a.wait_recv()
        add_rows(part, 256, [(part, 256), (v.other, 0)], 128)
        self.c = self.links.copy(rows(part, 256, 128), v.over, "far")
        part[384:512, :] = self.term(self.mine).astype(BF)

    def finish(self, out):
        part, v = self.v.terms, self.v
        self.b.wait_recv()
        add_rows(part, 384, [(part, 384), (v.near, 0)], 128)
        self.c.wait_recv()
        add_rows(out, 0, [(part, 384), (v.over, 0)], 128)
        self.links.settle(self.a, self.b, self.c)


class EightGather:
    def __init__(self, links, block, out, local, at):
        _, yl, _, yh, self.core = place()
        self.links, self.out = links, out
        self.y = yh * 2 + yl
        mine = self.spot(0)
        self.kept = keep(local, block, mine, at)
        self.a = links.copy(block, mine, "yp")
        self.b = links.copy(block, mine, "ym")
        self.last = [links.copy(block, mine, "twin")]

    def spot(self, step, at=0, count=128):
        return rows(self.out, (((self.y + step) % 4) * 2 + self.core) * 128 + at, count)

    def first(self):
        self.kept.wait()
        self.last[0].wait_recv()

    def sides(self):
        self.a.wait_recv()
        self.c = self.links.copy(self.spot(3, 0, 64), self.spot(3, 0, 64), "yp")
        self.last.append(self.links.copy(self.spot(3), self.spot(3), "twin"))
        self.b.wait_recv()
        self.d = self.links.copy(self.spot(1, 64, 64), self.spot(1, 64, 64), "ym")
        self.last.append(self.links.copy(self.spot(1), self.spot(1), "twin"))

    def far(self):
        self.c.wait_recv()
        self.d.wait_recv()
        self.last.append(self.links.copy(self.spot(2), self.spot(2), "twin"))

    def ready(self, at):
        self.last[at].wait_recv()


class EightReduce:
    def __init__(self, links, v):
        _, yl, _, yh, self.core = place()
        self.links, self.v = links, v
        self.y = yh * 2 + yl
        self.swaps = {}

    def send(self, step):
        y = (self.y + step) % 4
        for at in (0, 64):
            self.swaps[step, at] = self.links.copy(
                rows(self.v.terms, (y * 2 + 1 - self.core) * 128 + at, 64),
                rows(self.v.near8, y * 128 + at, 64),
                "twin",
            )

    def settle(self, step, at):
        self.swaps[step, at].wait_recv()
        y = (self.y + step) % 4
        near, first = self.v.near8, y * 128 + at
        add_rows(near, first, [(near, first), (self.v.terms, first + (y + self.core) * 128)], 64)

    def piece(self, step, at, count=64):
        return rows(self.v.near8, ((self.y + step) % 4) * 128 + at, count)

    def sides(self):
        copy, v = self.links.copy, self.v
        self.settle(1, 64)
        self.c = copy(self.piece(1, 64), rows(v.low8, 64, 64), "yp")
        self.settle(3, 0)
        self.d = copy(self.piece(3, 0), rows(v.high8, 0, 64), "ym")
        self.settle(1, 0)
        self.settle(3, 64)

    def start(self):
        copy, v = self.links.copy, self.v
        self.settle(2, 0)
        self.a = [copy(self.piece(2, at, 32), rows(v.one8, at, 32), "yp") for at in (0, 32)]
        self.settle(2, 64)
        self.b = [copy(self.piece(2, 64 + at, 32), rows(v.other8, at, 32), "ym") for at in (0, 32)]

    def forward(self):
        copy, v = self.links.copy, self.v
        self.last = []
        for at in (0, 32):
            self.a[at // 32].wait_recv()
            near = ((self.y + 1) % 4) * 128 + at
            add_rows(v.one8, at, [(v.one8, at), (v.near8, near)], 32)
            self.last.append(copy(rows(v.one8, at, 32), rows(v.low8, at, 32), "yp"))
            self.b[at // 32].wait_recv()
            near = ((self.y + 3) % 4) * 128 + 64 + at
            add_rows(v.other8, at, [(v.other8, at), (v.near8, near)], 32)
            self.last.append(copy(rows(v.other8, at, 32), rows(v.high8, 64 + at, 32), "ym"))

    def finish(self, out):
        self.settle(0, 0)
        self.settle(0, 64)
        for made in (self.c, self.d, *self.last):
            made.wait_recv()
        v = self.v
        add_rows(out, 0, [(v.near8, self.y * 128), (v.low8, 0), (v.high8, 0)], 128)


def half_tiles():
    for half in range(2):
        for at in range(7):
            width = 128 if at < 6 else HALF - 6 * 128
            yield half, half * HALF + at * 128, width, (at * 256, at * 256 + 128, CU + at * 128)


def pack(v, gains, query_weight, key_weight, value_weight, out_weight):
    tail = v.att_tail32
    tail[...] = jnp.zeros_like(tail)
    for at, piece in enumerate((query_weight, key_weight, value_weight, out_weight)):
        columns = slice(at * 256, (at + 1) * 256)
        v.att_main[:, columns] = piece[0:32, :]
        tail[at * 4 : at * 4 + 4, :256] = piece[32:36, :].astype(F32)
    for at, gain in enumerate(gains):
        width = gain.shape[1]
        tail[at : at + 1, 256 : 256 + width] = gain[...].astype(F32)
    v.att_tail[...] = tail[...].astype(BF)


def pack_ffn(v, pieces, chosen):
    if 0 in chosen:
        v.ffn_main[...] = jnp.zeros_like(v.ffn_main)
        v.ffn_tail32[...] = jnp.zeros_like(v.ffn_tail32)
    for half, first, width, targets in half_tiles():
        columns = slice(first, first + width)
        for at in chosen:
            piece, target = pieces[at], targets[at]
            v.ffn_main[half, :, target : target + width] = piece[0:32, columns]
            row, lane = half * 16 + target // HPAD * 4, target % HPAD
            v.ffn_tail32[row : row + 4, lane : lane + width] = piece[32:36, columns].astype(F32)
    if 2 in chosen:
        for half in range(2):
            v.ffn_tail[half] = v.ffn_tail32[half * 16 : half * 16 + 16, :].astype(BF)


def make_shuffle(v):
    place_at = lax.broadcasted_iota(jnp.int32, (1, D), 1)
    slot = jnp.where(place_at < 1024, place_at >> 5, (place_at - 1024) >> 2)
    inside = jnp.where(place_at < 1024, place_at & 31, 32 + (place_at & 3))
    part, outer, inner = slot >> 4, (slot >> 2) & 3, slot & 3
    owner = jnp.where(part == 0, outer * 8 + inner, inner * 8 + 4 + outer)
    natural = owner * 36 + inside

    @pl.loop(0, D, step=128)
    def _(at):
        row = lax.broadcasted_iota(jnp.int32, (128, D), 0) + at
        v.shuffle[chunk_rows(at, 128), :] = (row == natural).astype(F32).astype(BF)


def make_tables(v, lengths):
    @pl.loop(0, 512, step=64)
    def _(at):
        here = chunk_rows(at, 64)
        token = lax.broadcasted_iota(jnp.int32, (64, 128), 0) + at
        lane = lax.broadcasted_iota(jnp.int32, (64, 128), 1)
        begin, end = jnp.zeros((64, 128), jnp.int32), 0
        for document in range(8):
            end = end + lengths[0, document]
            begin = jnp.where(token >= end, end, begin)
        angle = (token - begin).astype(F32) * jnp.exp(
            lane.astype(F32) * (-2.0 * math.log(THETA) / 256)
        )
        v.begins[here, :] = begin
        v.cosine[here, :] = jnp.cos(angle)
        v.sine[here, :] = jnp.sin(angle)


def layer_kernel(
    tokens_in,
    lengths,
    att_in_gain,
    query_weight,
    key_weight,
    value_weight,
    query_gain,
    key_gain,
    out_weight,
    att_out_gain,
    ffw_in_gain,
    gate_weight,
    up_weight,
    down_weight,
    ffw_out_gain,
    cotangent_in,
    mixed_out,
    tokens_out,
    att_sum,
    att_tail_sum,
    gate_up_sum,
    down_sum,
    ffn_tail_sum,
    *refs,
):
    v = SimpleNamespace(**dict(zip(NAMES, refs)))
    local, send, recv = refs[len(NAMES) :]
    tokens, cotangent, cosine, sine_part, begins = (
        v.tokens,
        v.cotangent,
        v.cosine,
        v.sine,
        v.begins,
    )
    v.sb = v.ab.at[pl.ds(0, 512), pl.ds(0, 512)]
    v.qkvb = v.ab.at[pl.ds(0, 512), pl.ds(512, 768)]
    v.attb = v.ab.at[pl.ds(0, 512), pl.ds(1280, 256)]
    met = greet(("ap", "am", "ao", "bp", "bm", "bo", "pair", "yp", "ym") + GROUP)
    gain_refs = (att_in_gain, att_out_gain, ffw_in_gain, ffw_out_gain, query_gain, key_gain)
    pack(v, gain_refs, query_weight, key_weight, value_weight, out_weight)
    met()
    links = Links(send, recv)
    _, yl, _, yh, core = place()
    sites = roles()

    first_columns, last_columns = pl.ds(0, CU), pl.ds(CU, HPAD)
    bufs = (
        (v.watt, MAIN),
        (v.tatt, TAIL),
        (v.wffn.at[:, first_columns], MAIN),
        (v.wffn.at[:, last_columns], MAIN),
        (v.tffn, TAIL),
    )
    firsts, theirs = [
        (
            v.att_main,
            v.att_tail,
            v.ffn_main.at[half, :, first_columns],
            v.ffn_main.at[half, :, last_columns],
            v.ffn_tail.at[half],
        )
        for half in (yl, 1 - yl)
    ]
    own = sites[0][0] + sites[0][1] * 4 + sites[0][2]
    kept, swaps = {}, {}
    inners, outers = {}, {}

    def launch(at):
        ref, unit = bufs[at]
        target = rows(ref, own * unit, unit)
        kept[at] = keep(local, firsts[at], target, at)
        swaps[at] = links.copy(theirs[at], target, "pair")

    def spread(at, role, level):
        ref, unit = bufs[at]
        kind = SpreadAtOnce if unit == TAIL else Spread
        start, outer, inner, outer_sides, inner_sides = sites[role]
        if level == 1:
            first = lambda i: (start + outer * 4 + i) * unit
            inners[at, role] = kind(links, ref, first, inner, unit, 16, *inner_sides)
        else:
            first = lambda o: (start + o * 4) * unit
            outers[at, role] = kind(links, ref, first, outer, 4 * unit, 2 * unit, *outer_sides)

    att_jobs = [(at, role) for at in (1, 0) for role in range(2)]
    ffn_jobs = [(at, role) for at in (2, 4, 3) for role in range(2)]
    for at in (1, 0):
        launch(at)
    for at in (1, 0):
        kept[at].wait()
        spread(at, 0, 1)
    pieces = (gate_weight, up_weight, down_weight)
    pack_ffn(v, pieces, (0, 1))
    launch(2)
    pack_ffn(v, pieces, (2,))
    launch(4)
    launch(3)
    for at in (1, 0):
        swaps[at].wait_recv()
        spread(at, 1, 1)
    inners[0, 0].forward()
    for at in (2, 4, 3):
        kept[at].wait()
        spread(at, 0, 1)
    inners[0, 1].forward()
    make_shuffle(v)
    tokens[...] = matmul(tokens_in[...], v.shuffle[...]).astype(BF)
    raw_gather = FourGather(links, tokens, v.raw, local, 5)
    for job in att_jobs:
        inners[job].finish()
        spread(*job, 0)
    for at in (2, 4, 3):
        swaps[at].wait_recv()
        spread(at, 1, 1)
    for at in (2, 3):
        inners[at, 0].forward()
    make_gain_maps(v)
    raw_gather.forward()
    for at in (2, 3):
        inners[at, 1].forward()
    for job in att_jobs:
        outers[job].forward()
    for job in ffn_jobs:
        inners[job].finish()
        spread(*job, 0)
    make_tables(v, lengths)
    cotangent[...] = matmul(cotangent_in[...], v.shuffle[...]).astype(BF)
    for job in att_jobs[:2]:
        outers[job].finish()

    gains, ggains = v.gains, v.ggains
    for chunk in range(4):
        here = slice(chunk * 128, (chunk + 1) * 128)
        spreaded = right_inner(v.tatt[here, 256:], v.fold[...])
        term = matmul(row_picks(), (spreaded * v.masks[here, :].astype(F32)).astype(BF))
        gains[...] = term if chunk == 0 else gains[...] + term
    gains[...] = gains[...] + 1.0
    ggains[...] = jnp.zeros_like(ggains)
    raw_gather.finish()

    @pl.loop(0, 512, step=128)
    def _(at):
        vector = v.raw[chunk_rows(at, 128), :].astype(F32)
        v.rows1[chunk_rows(at, 128), :] = (vector * root(vector) * gains[0:1, :D]).astype(BF)

    for job in att_jobs[2:]:
        outers[job].finish()
    for at in range(4):
        v.watt[1024:, at * 256 : (at + 1) * 256] = matmul(
            tail_picks(at), v.tatt[:, :256]
        ).astype(BF)

    @pl.loop(0, 512, step=128)
    def _(at):
        here = chunk_rows(at, 128)
        made = matmul(v.rows1[here, :], v.watt[:, :768])
        v.vb[here, :] = made[:, 512:].astype(BF)
        v.qkraw[here, :] = made[:, :512]
        cos, sin = cosine[here, :], sine_part[here, :]
        query, key = made[:, :256], made[:, 256:512]
        query = turn(query * root(query) * gains[4:5, D:], cos, sin) * (1.0 / 16.0)
        v.qb[here, :] = query.astype(BF)
        v.kb[here, :] = turn(key * root(key) * gains[5:6, D:], cos, sin).astype(BF)

    for job in ffn_jobs[:4]:
        outers[job].forward()
    for chunk in range(4):
        first, last = chunk * 128, (chunk + 1) * 128
        scores = right_inner(v.qb[first:last, :], v.kb[:last, :])
        key_at = lax.broadcasted_iota(jnp.int32, (128, last), 1)
        query_at = lax.broadcasted_iota(jnp.int32, (128, last), 0) + first
        allowed = (key_at <= query_at) & (key_at >= begins[first:last, :1])
        scores = jnp.where(allowed, scores, NEGATIVE)
        powers = jnp.exp(scores - jnp.max(scores, axis=1, keepdims=True))
        shares = powers / jnp.sum(powers, axis=1, keepdims=True)
        v.prob[first:last, :last] = shares
        if last < 512:
            v.prob[first:last, last:] = jnp.zeros((128, 512 - last), F32)
        v.attd[first:last, :] = matmul(shares.astype(BF), v.vb[:last, :]).astype(BF)
    reduced = FourReduce(
        links,
        lambda t: right_inner(v.attd[chunk_rows(t * 128, 128), :], v.watt[:, 768:]),
        v,
    )
    reduced.middle()
    for job in ffn_jobs[4:]:
        outers[job].forward()
    reduced.finish(v.attraw)

    @pl.loop(0, 128, step=64)
    def _(at):
        here = chunk_rows(at, 64)
        term = v.attraw[here, :]
        total = tokens[here, :].astype(F32) + term * root(term) * gains[1:2, :D]
        v.middle[here, :] = total
        v.block[here, :] = (total * root(total) * gains[2:3, :D]).astype(BF)

    gathered = EightGather(links, v.block, v.rows2, local, 6)
    for job in ffn_jobs[:4]:
        outers[job].finish()
    for at in range(2):
        v.wffn[1024:, at * HPAD : (at + 1) * HPAD] = matmul(tail_picks(at), v.tffn[...]).astype(BF)
    y = yh * 2 + yl

    def forward(step):
        here = chunk_rows(((y + step) % 4) * 256, 256)
        former = v.rows2[here, :]
        for at in range(7):
            both = matmul(former, v.wffn[:, at * 256 : (at + 1) * 256])
            gate, up = both[:, :128], both[:, 128:]
            square = gate * gate
            bend = jnp.tanh(gate * (GELU + GELU * 0.044715 * square))
            half = 0.5 + 0.5 * bend
            active = gate * half
            slope = half + (0.5 - 0.5 * bend * bend) * gate * (
                GELU + GELU * 3.0 * 0.044715 * square
            )
            v.ab[here, at * 256 : at * 256 + 128] = (up * slope).astype(BF)
            v.ab[here, at * 256 + 128 : at * 256 + 256] = active.astype(BF)
            v.hid[here, at * 128 : at * 128 + 128] = (active * up).astype(BF)

    def lower(step):
        here = chunk_rows(((y + step) % 4) * 256, 256)
        v.terms[here, :] = right_inner(v.hid[here, :], v.wffn[:, CU:]).astype(BF)

    def backward(step):
        here = chunk_rows(((y + step) % 4) * 256, 256)
        slopes = matmul(v.back[here, :], v.wffn[:, CU:])
        for at in range(7):
            slope = slopes[:, at * 128 : (at + 1) * 128]
            for side in range(2):
                columns = slice(at * 256 + side * 128, at * 256 + side * 128 + 128)
                v.ab[here, columns] = (v.ab[here, columns].astype(F32) * slope).astype(BF)

    def raise_up(step):
        here = chunk_rows(((y + step) % 4) * 256, 256)
        v.terms[here, :] = right_inner(v.ab[here, :], v.wffn[:, :CU]).astype(BF)

    reduced = EightReduce(links, v)
    gathered.first()
    forward(0)
    gathered.sides()
    gathered.ready(1)
    forward(3)
    gathered.far()
    gathered.ready(2)
    forward(1)
    for job in ffn_jobs[4:]:
        outers[job].finish()
    v.wffn[1024:, CU:] = matmul(tail_picks(2), v.tffn[...]).astype(BF)
    for step in (0, 3, 1):
        lower(step)
        reduced.send(step)
    gathered.ready(3)
    forward(2)
    reduced.sides()
    lower(2)
    reduced.send(2)
    reduced.start()
    reduced.forward()
    reduced.finish(v.summed)
    links.drain()

    @pl.loop(0, 128, step=64)
    def _(at):
        here = chunk_rows(at, 64)
        term, grad = v.summed[here, :], cotangent[here, :].astype(F32)
        v.other[here, :] = (v.middle[here, :] + term * root(term) * gains[3:4, :D]).astype(BF)
        term_grad, gain_grad = norm_back(term, gains[3:4, :D], grad)
        v.block[here, :] = term_grad.astype(BF)
        ggains[3:4, :D] += gain_grad

    grads = (
        v.gatt,
        v.tatt,
        v.wffn.at[:, pl.ds(0, CU)],
        v.gdown,
        v.tffn,
    )
    collects = {}

    def room(at, *numbers):
        return getattr(v, "room%d%d%d" % (at, *numbers))

    def collect(at, role, level):
        unit = KINDS[at][0]
        kind = CollectAtOnce if unit == TAIL else Collect
        start, outer, inner, outer_sides, inner_sides = sites[role]
        rooms = [room(at, role * 2 + level, side) for side in range(4)]
        if level == 0:
            first = lambda o: (start + o * 4) * unit
            made = kind(
                links, grads[at], first, outer, 4 * unit, 2 * unit, *outer_sides, rooms
            )
        else:
            first = lambda i: i * unit
            ref = room(at, role * 2, 2)
            made = kind(links, ref, first, inner, unit, 16, *inner_sides, rooms)
        collects[at, role, level] = made

    def both(work, at, *level):
        for role in range(2):
            work(at, role, *level)

    def pass_on(at, role, level):
        collects[at, role, level].forward()

    def turn_in(at, role):
        collects[at, role, 0].finish(room(at, role * 2, 2), 0)
        collect(at, role, 1)

    sums = [getattr(v, "sum%d" % at) for at in range(5)]
    others = [getattr(v, "swap%d" % at) for at in range(5)]

    def swap(at):
        unit = KINDS[at][0]
        for role in range(2):
            collects[at, role, 1].finish(sums[at], role * unit)
        return links.copy(rows(sums[at], unit, unit), others[at], "pair")

    gathered = EightGather(links, v.block, v.back, local, 7)
    mixed_out[...] = right_inner(v.other[...], v.shuffle[...]).astype(BF)
    reduced = EightReduce(links, v)
    gathered.first()
    backward(0)
    raise_up(0)
    reduced.send(0)
    gathered.sides()
    gathered.ready(1)
    backward(3)
    raise_up(3)
    reduced.send(3)
    gathered.far()
    gathered.ready(2)
    backward(1)
    raise_up(1)
    reduced.send(1)
    gathered.ready(3)
    columns_of = [slice(at * 384, (at + 1) * 384) for at in range(3)]
    for columns in columns_of:
        v.gdown[columns, :] = left_inner(v.back[:, columns], v.hid[...]).astype(BF)
    both(collect, 3, 0)
    reduced.sides()
    backward(2)
    raise_up(2)
    reduced.send(2)
    reduced.start()
    both(pass_on, 3, 0)

    def raised(columns):
        v.wffn[columns, :CU] = left_inner(v.rows2[:, columns], v.ab[...]).astype(BF)

    raised(columns_of[0])
    raised(columns_of[1])
    reduced.forward()
    raised(columns_of[2])
    both(collect, 2, 0)
    total = None
    for at, piece in enumerate((v.wffn[1024:, :HPAD], v.wffn[1024:, HPAD:CU], v.gdown[1024:, :])):
        term = left_inner(tail_picks(at), piece)
        total = term if at == 0 else total + term
    v.tffn[...] = total.astype(BF)
    both(collect, 4, 0)
    both(turn_in, 3)
    reduced.finish(v.summed)
    links.settle(gathered.a, gathered.b, gathered.last[0], *reduced.swaps.values())

    @pl.loop(0, 128, step=64)
    def _(at):
        here = chunk_rows(at, 64)
        grad = cotangent[here, :].astype(F32)
        more, gain_grad = norm_back(v.middle[here, :], gains[2:3, :D], v.summed[here, :])
        ggains[2:3, :D] += gain_grad
        total = grad + more
        v.midgrad[here, :] = total
        term_grad, gain_grad = norm_back(v.attraw[here, :], gains[1:2, :D], total)
        ggains[1:2, :D] += gain_grad
        v.block[here, :] = term_grad.astype(BF)

    att_back = FourGather(links, v.block, v.raw, local, 8)
    both(pass_on, 3, 1)
    att_back.forward()
    att_back.finish()
    both(pass_on, 2, 0)

    @pl.loop(0, 512, step=128)
    def _(at):
        here = chunk_rows(at, 128)
        v.attb[here, :] = matmul(v.raw[here, :], v.watt[:, 768:]).astype(BF)

    for chunk in range(4):
        first, last = chunk * 128, (chunk + 1) * 128
        shares_grad = right_inner(v.attb[first:last, :], v.vb[:last, :])
        shares = v.prob[first:last, :last]
        inner = jnp.sum(shares * shares_grad, axis=1, keepdims=True)
        v.sb[first:last, :last] = (shares * (shares_grad - inner)).astype(BF)
        if last < 512:
            v.sb[first:last, last:] = jnp.zeros((128, 512 - last), BF)
    v.qkvb[:, 512:] = left_inner(v.prob[...].astype(BF), v.attb[...]).astype(BF)
    query_grad = matmul(v.sb[...], v.kb[...]) * (1.0 / 16.0)
    key_grad = left_inner(v.sb[...], v.qb[...])
    for side, rotated in enumerate((query_grad, key_grad)):
        columns = slice(side * 256, (side + 1) * 256)
        plain = turn(rotated, cosine[...], -sine_part[...])
        made, gain_grad = norm_back(v.qkraw[:, columns], gains[4 + side : 5 + side, D:], plain)
        v.qkvb[:, columns] = made.astype(BF)
        ggains[4 + side : 5 + side, D:] = gain_grad
    reduced = FourReduce(
        links,
        lambda t: right_inner(v.qkvb[chunk_rows(t * 128, 128), :], v.watt[:, :768]),
        v,
    )
    both(turn_in, 2)
    both(turn_in, 4)
    for at in range(3):
        columns = slice(at * 384, (at + 1) * 384)
        v.gatt[columns, :768] = left_inner(v.rows1[:, columns], v.qkvb[...]).astype(BF)
        v.gatt[columns, 768:] = left_inner(v.raw[:, columns], v.attd[...]).astype(BF)
    both(collect, 0, 0)
    both(pass_on, 2, 1)
    reduced.middle()
    swapped = {at: swap(at) for at in (3, 2, 4)}
    both(pass_on, 0, 0)
    total = None
    for at in range(4):
        term = left_inner(tail_picks(at), v.gatt[1024:, at * 256 : (at + 1) * 256])
        total = term if at == 0 else total + term
    v.tatt[:, :256] = total.astype(BF)
    reduced.finish(v.summed)

    @pl.loop(0, 128, step=64)
    def _(at):
        here = chunk_rows(at, 64)
        made, gain_grad = norm_back(
            tokens[here, :].astype(F32), gains[0:1, :D], v.summed[here, :]
        )
        v.midgrad[here, :] += made
        ggains[0:1, :D] += gain_grad

    wide = left_inner(row_picks(), ggains[...].astype(BF))
    for chunk in range(4):
        here = slice(chunk * 128, (chunk + 1) * 128)
        v.tatt[here, 256:] = matmul(
            (wide * v.masks[here, :].astype(F32)).astype(BF), v.fold[...]
        ).astype(BF)
    both(collect, 1, 0)
    both(turn_in, 0)
    both(turn_in, 1)
    both(pass_on, 0, 1)
    high = v.midgrad[...].astype(BF)
    low = (v.midgrad[...] - high.astype(F32)).astype(BF)
    tokens_out[...] = right_inner(high, v.shuffle[...]) + right_inner(low, v.shuffle[...])
    def share(ref, room, unit):
        copies = []
        for at, name in enumerate(GROUP):
            source = ref.at[pl.ds(unit if at > 2 else 0, unit), :]
            copies.append(links.copy(source, rows(room, at * unit, unit), name))
        return copies

    swapped[1] = swap(1)
    shared = share(sums[1], v.shared_tail, TAIL)
    swapped[0] = swap(0)
    shared += share(sums[0].at[:, pl.ds(256, 512)], v.shared, MAIN)
    outs = ((3, down_sum), (2, gate_up_sum), (4, ffn_tail_sum))
    for at, out in outs:
        unit = KINDS[at][0]
        add_rows(out, yl * unit, [(sums[at], 0)], unit)
        swapped[at].wait_recv()
        add_rows(out, (1 - yl) * unit, [(others[at], 0)], unit)
    swapped[0].wait_recv()
    add_rows(att_sum, 0, [(sums[0], 0), (others[0], 0)], MAIN)
    swapped[1].wait_recv()
    add_rows(att_tail_sum, 0, [(sums[1], 0), (others[1], 0)], TAIL)
    for made in shared:
        made.wait_recv()
    total, total_tail = att_sum[:, 256:768], att_tail_sum[...]
    for at in range(6):
        total = total + v.shared[at * MAIN : (at + 1) * MAIN, :].astype(F32)
        total_tail = total_tail + v.shared_tail[at * TAIL : (at + 1) * TAIL, :].astype(F32)
    att_sum[:, 256:768] = total
    row = lax.broadcasted_iota(jnp.int32, (TAIL, TA), 0)
    column = lax.broadcasted_iota(jnp.int32, (TAIL, TA), 1)
    common = (column >= 256) | ((row >= 4) & (row < 12))
    att_tail_sum[...] = jnp.where(common, total_tail, att_tail_sum[...])
    links.drain()


def unpack_kernel(*refs):
    fetched, sems = refs[:7], refs[-1]
    (
        mixed_out,
        tokens_out,
        att_in_out,
        query_out,
        key_out,
        value_out,
        query_gain_out,
        key_gain_out,
        out_out,
        att_out_out,
        ffw_in_out,
        gate_out,
        up_out,
        down_out,
        ffw_out_out,
    ) = refs[7:22]
    att_sum, att_tail_sum, gate_up_sum, down_sum, ffn_tail_sum = refs[22:27]
    targets = (mixed_out, tokens_out) + refs[22:27]
    made = [
        pltpu.make_async_copy(source, target, sems.at[at])
        for at, (source, target) in enumerate(zip(fetched, targets))
    ]
    for copy in made:
        copy.start()
    for copy in made:
        copy.wait()
    for half, first, width, sources in half_tiles():
        columns = slice(first, first + width)
        main = slice(half * 32, half * 32 + 32)
        for out, source, ref in (
            (gate_out, sources[0], gate_up_sum),
            (up_out, sources[1], gate_up_sum),
            (down_out, sources[2], down_sum),
        ):
            row, lane = half * 16 + source // HPAD * 4, source % HPAD
            at = source % CU if ref is gate_up_sum else source - CU
            out[0:32, columns] = ref[main, at : at + width]
            out[32:36, columns] = ffn_tail_sum[row : row + 4, lane : lane + width]
    for at, out in enumerate((query_out, key_out, value_out, out_out)):
        out[0:32, :] = att_sum[:, at * 256 : (at + 1) * 256]
        out[32:36, :] = att_tail_sum[at * 4 : at * 4 + 4, :256]
    gain_outs = (att_in_out, att_out_out, ffw_in_out, ffw_out_out, query_gain_out, key_gain_out)
    for at, out in enumerate(gain_outs):
        out[...] = att_tail_sum[at : at + 1, 256 : 256 + out.shape[1]]


VM = pl.BlockSpec(memory_space=pltpu.VMEM)
COPIES = 300


def layer(*operands):
    sums = [
        ((128, D), BF),
        ((128, D), F32),
        ((MAIN, CA), F32),
        ((TAIL, TA), F32),
        ((2 * MAIN, CU), F32),
        ((2 * MAIN, HPAD), F32),
        ((2 * TAIL, HPAD), F32),
    ]
    outs = [
        ((128, D), BF),
        ((128, D), F32),
        ((1, 36), F32),
        ((36, 256), F32),
        ((36, 256), F32),
        ((36, 256), F32),
        ((1, 8), F32),
        ((1, 8), F32),
        ((36, 256), F32),
        ((1, 36), F32),
        ((1, 36), F32),
        ((36, 1728), F32),
        ((36, 1728), F32),
        ((36, 1728), F32),
        ((1, 36), F32),
    ]
    made = pl.pallas_call(
        layer_kernel,
        out_shape=[jax.ShapeDtypeStruct(*out) for out in sums],
        in_specs=[VM, pl.BlockSpec(memory_space=pltpu.SMEM)] + [VM] * 14,
        out_specs=[VM] * len(sums),
        scratch_shapes=[pltpu.VMEM(*SHAPES[name]) for name in NAMES]
        + [pltpu.SemaphoreType.DMA((9,))]
        + [pltpu.SemaphoreType.DMA((COPIES,))] * 2,
        compiler_params=pltpu.CompilerParams(
            collective_id=0, has_side_effects=True, vmem_limit_bytes=LIMIT
        ),
    )
    unpack = pl.pallas_call(
        unpack_kernel,
        out_shape=[jax.ShapeDtypeStruct(*out) for out in outs],
        in_specs=[pl.BlockSpec(memory_space=pl.ANY)] * len(sums),
        out_specs=[VM] * len(outs),
        scratch_shapes=[pltpu.VMEM(*shape) for shape in sums[2:]]
        + [pltpu.SemaphoreType.DMA((len(sums),))],
        compiler_params=pltpu.CompilerParams(vmem_limit_bytes=LIMIT),
    )
    return unpack(*made(*operands))


def shards(*arguments):
    operands = list(arguments)
    for at in (8, 13):
        operands[at] = operands[at].T
    made = list(layer(*[array[None] if array.ndim == 1 else array for array in operands]))
    for at in (8, 13):
        made[at] = made[at].T
    return tuple(array[0] if array.shape[0] == 1 else array for array in made)


def solution(mesh):
    return jax.shard_map(
        shards,
        mesh=mesh,
        in_specs=(
            P(("dp", "tensor"), None),
            P("dp", None),
            P("dp"),
            P("dp", "tensor"),
            P("dp", None),
            P("dp", None),
            P("dp"),
            P("dp"),
            P("tensor", "dp"),
            P("dp"),
            P("dp"),
            P("dp", "tensor"),
            P("dp", "tensor"),
            P("tensor", "dp"),
            P("dp"),
            P(("dp", "tensor"), None),
        ),
        out_specs=(
            P(("dp", "tensor"), None),
            P(("dp", "tensor"), None),
            P("dp"),
            P("dp", "tensor"),
            P("dp", None),
            P("dp", None),
            P("dp"),
            P("dp"),
            P("tensor", "dp"),
            P("dp"),
            P("dp"),
            P("dp", "tensor"),
            P("dp", "tensor"),
            P("tensor", "dp"),
            P("dp"),
        ),
        check_vma=False,
    )
```
